256 devices in a mesh: aux: 16 (over y, x_lo, core), bas: 16 (over z, x_hi).
Axes of the slice: x: 4 (x_hi: 2, x_lo: 2; x = x_hi * 2 + x_lo), y: 4, z: 8, core: 2. Of those that a mesh axis runs over, the one named last changes fastest.
Arguments:
- factors: float32 [16, 8192, 1024], P('aux', 'bas'), may hold values from -0.8 to 0.8
Outputs:
- k_tiles: float32 [16, 512, 9, 512], P('bas', 'aux')
The draws below stay inside these ranges and needn't reach their ends.
All inputs are finite; a program needn't handle non-finite values.
Results may differ from the reference program's by a relative error of at most 0.0003.
Values sent between devices are 32-bit elements; how exact they have to be, the bound alone decides.
No kernel may reach another device: no remote copies, remote signals or barrier semaphores. Data moves between devices by JAX's collectives and lax.ppermute only.
A program may use at most 128 MiB of HBM per device.

```python
import jax
import jax.numpy as jnp
from jax import lax

NBF = 8192
NOCC = 1024
QAUX = 16
NBLK = 16
TILE = 512
OFFS = 9


def spiked(drawn, rng, source, target, parts, factor):
    owner, partner = [(jnp.arange(drawn.shape[position]) // (drawn.shape[position] // parts)).reshape([-1 if axis == position else 1 for axis in range(drawn.ndim)]) for position in (source, target)]
    chosen = jax.random.permutation(rng, parts)[partner]
    strong = (owner == chosen) | (owner == (partner + parts // 2) % parts)
    return jnp.where(strong, factor * drawn, drawn)


def block_scale(own_key, dims, split, least, top_value):
    level = 1.0
    for axis_at, shards_of in split:
        heights = jax.random.uniform(jax.random.fold_in(jax.random.fold_in(own_key, 6), axis_at), (shards_of,), jnp.float32, least / len(split), top_value / len(split))
        level = level * jnp.repeat(jnp.exp(heights), dims[axis_at] // shards_of).reshape((-1,) + (1,) * (len(dims) - 1 - axis_at))
    return level


def noise_with(own_key, dims, scale, bound, shards, heavy, kind=jnp.bfloat16):
    values = scale * jax.random.normal(own_key, dims, jnp.float32)
    if shards:
        values = values * block_scale(own_key, dims, shards, -0.22, 0.18)
    return jnp.clip(spiked(values, jax.random.fold_in(own_key, 3), *heavy), -bound, bound).astype(kind)


def setup_inputs(seed: int = 0) -> dict:
    keys = jax.random.split(jax.random.key(seed), 2)
    return {
        "factors": noise_with(keys[0], (QAUX, NBF, NOCC), 0.1, 0.8, ((0, 16), (1, 16)), (0, 1, 16, 2.0), jnp.float32),
    }


def reference(factors):
    doubled = jnp.concatenate([factors, factors], axis=1)

    def one_block(index):
        start = (index * TILE).astype(jnp.int32)
        own_rows = lax.dynamic_slice_in_dim(factors, start, TILE, 1)
        columns = lax.dynamic_slice_in_dim(doubled, start, OFFS * TILE, 1)
        tiles = jnp.einsum("qmi,qni->mn", own_rows, columns, precision=lax.Precision.HIGHEST, preferred_element_type=jnp.float32)
        return tiles.reshape(TILE, OFFS, TILE)

    return lax.map(one_block, jnp.arange(NBLK, dtype=jnp.int32))
```

```python
import jax
import jax.numpy as jnp
from jax import lax
from jax.sharding import PartitionSpec as P

NY, NXL, NC, NZ, NXH = 4, 2, 2, 8, 2
TILE = 512
SHARE = 32


def place(y, xl, c, z, xh):
    return (((y % NY) * NXL + xl % NXL) * NC + c % NC) * (NZ * NXH) + (z % NZ) * NXH + xh % NXH


def send(value, target):
    pairs = []
    for y in range(NY):
        for xl in range(NXL):
            for c in range(NC):
                for z in range(NZ):
                    for xh in range(NXH):
                        to = target(y, xl, c, z, xh)
                        if to is not None:
                            pairs.append((place(y, xl, c, z, xh), place(*to)))
    return lax.ppermute(value, ("aux", "bas"), pairs)


def z_by(step):
    return lambda y, xl, c, z, xh: (y, xl, c, z + step, xh)


def y_by(step):
    return lambda y, xl, c, z, xh: (y + step, xl, c, z, xh)


def swap_core(y, xl, c, z, xh):
    return y, xl, 1 - c, z, xh


def swap_xh(y, xl, c, z, xh):
    return y, xl, c, z, 1 - xh


def first_to_second(y, xl, c, z, xh):
    return (y, xl, c, z, 1) if xh == 0 else None


def dot(rows, columns):
    return lax.dot_general(
        rows,
        columns,
        (((1,), (1,)), ((), ())),
        precision=lax.Precision.HIGH,
        preferred_element_type=jnp.float32,
    )


def pick(value, index, axis):
    return lax.dynamic_index_in_dim(value, index, axis, keepdims=False)


def summed(partial_value, moves, y, xl, c):
    width = partial_value.shape[-1]
    v = partial_value.reshape(NY * NXL, NC, SHARE, width)
    got = send(pick(v, 1 - c, 1), swap_core)
    v = (pick(v, c, 1) + got).reshape(NY, NXL * SHARE, width)
    got = [send(pick(v, (y + r) % NY, 0), y_by(r)) for r in (1, 3, 2)]
    v = (pick(v, y, 0) + got[0] + got[1] + got[2]).reshape(NXL, SHARE, width)
    mine, other = pick(v, xl, 0), pick(v, 1 - xl, 0)
    tiles = []
    at = 0
    while at < len(moves):
        end = at
        while end < len(moves) and moves[end] == moves[at]:
            end += 1
        shift = moves[at]
        part = slice(at * TILE, end * TILE)
        got = send(other[:, part], lambda y, xl, c, z, xh: (y, 1 - xl, c, z + shift[xh], xh))
        kept = mine[:, part]
        if shift != (0, 0):
            kept = send(kept, lambda y, xl, c, z, xh: (y, xl, c, z + shift[xh], xh))
        tiles += jnp.split(kept + got, end - at, axis=1)
        at = end
    return tiles


def body(factors):
    aux, bas = lax.axis_index("aux"), lax.axis_index("bas")
    y, xl, c, xh = aux // 4, (aux // 2) % 2, aux % 2, bas % 2
    first = xh == 0
    own = factors[0]
    halves = [own[:256], own[256:]]
    up1 = [send(v, z_by(-1)) for v in halves]
    dn1 = [send(v, z_by(1)) for v in halves]
    up2 = [send(v, z_by(-1)) for v in up1]
    dn2 = [send(v, z_by(1)) for v in dn1]
    ot1 = [send(v, swap_xh) for v in up1]
    ot2 = [send(v, first_to_second) for v in up2]
    p1, m1, p2, m2, o1, o2 = (jnp.concatenate(v, 0) for v in (up1, dn1, up2, dn2, ot1, ot2))

    g1 = jnp.concatenate([dot(own, own), dot(own, p1), dot(m1, p1)], 1)
    d0, d1, d2 = summed(g1, [(0, 0), (0, 0), (-1, -1)], y, xl, c)
    g2 = jnp.concatenate([dot(jnp.where(first, p1, own), o1), dot(jnp.where(first, own, m1), o1)], 1)
    ta, tb = summed(g2, [(1, 0), (0, -1)], y, xl, c)
    g3 = jnp.concatenate([dot(jnp.where(first, m1, m2), o1), dot(m1, p2), dot(m2, p2)], 1)
    tc, d3, d4 = summed(g3, [(-1, -2), (-1, -1), (-2, -2)], y, xl, c)
    g4 = dot(m2, jnp.where(first, o1, o2))
    (td,) = summed(g4, [(-2, -2)], y, xl, c)
    return jnp.stack([d0, ta, d1, tb, d2, tc, d3, td, d4], axis=1)[None]


def solution(mesh):
    return jax.shard_map(
        body,
        mesh=mesh,
        in_specs=(P("aux", "bas", None),),
        out_specs=P("bas", "aux", None, None),
        check_vma=False,
    )
```

```python
import functools

import jax
import jax.numpy as jnp
from jax import lax
from jax.experimental import pallas as pl
from jax.experimental.pallas import tpu as pltpu
from jax.sharding import PartitionSpec as P

NY, NXL, NC, NZ, NXH = 4, 2, 2, 8, 2
TILE = 512
SHARE = 32


def place(y, xl, c, z, xh):
    return (((y % NY) * NXL + xl % NXL) * NC + c % NC) * (NZ * NXH) + (z % NZ) * NXH + xh % NXH


def send(value, target):
    pairs = []
    for y in range(NY):
        for xl in range(NXL):
            for c in range(NC):
                for z in range(NZ):
                    for xh in range(NXH):
                        to = target(y, xl, c, z, xh)
                        if to is not None:
                            pairs.append((place(y, xl, c, z, xh), place(*to)))
    return lax.ppermute(value, ("aux", "bas"), pairs)


def z_by(step):
    return lambda y, xl, c, z, xh: (y, xl, c, z + step, xh)


def y_by(step):
    return lambda y, xl, c, z, xh: (y + step, xl, c, z, xh)


def swap_core(y, xl, c, z, xh):
    return y, xl, 1 - c, z, xh


def swap_xh(y, xl, c, z, xh):
    return y, xl, c, z, 1 - xh


def call(kernel, outs, args, vmem, scratch=()):
    return pl.pallas_call(
        kernel,
        out_shape=[jax.ShapeDtypeStruct(shape, jnp.float32) for shape in outs],
        in_specs=[pl.BlockSpec(memory_space=pltpu.SMEM)] + [pl.BlockSpec(memory_space=pltpu.VMEM)] * (len(args) - 1),
        out_specs=[pl.BlockSpec(memory_space=pltpu.VMEM)] * len(outs),
        scratch_shapes=list(scratch),
        compiler_params=pltpu.CompilerParams(vmem_limit_bytes=vmem * 2**20),
        cost_estimate=pl.CostEstimate(flops=0, bytes_accessed=0, transcendentals=0),
    )(*args)


def two_terms(value):
    high = value.astype(jnp.bfloat16)
    return high, (value - high.astype(jnp.float32)).astype(jnp.bfloat16)


def products_kernel(tiles, rows, columns, count, before, place_ref, *refs):
    operands, (mine, other, row_high, row_low, column_high, column_low) = refs[:count], refs[-6:]
    y, xl, c, xh = (place_ref[i] for i in range(4))

    def split(block, high, low, i, target):
        done = 0
        for at in block:
            chunk = operands[at]
            groups = chunk.shape[0] // SHARE

            @pl.loop(0, groups)
            def _(g, chunk=chunk, done=done):
                to = pl.ds(pl.multiple_of(target(g + done) * SHARE, SHARE), SHARE)
                value = chunk[pl.ds(pl.multiple_of(g * SHARE, SHARE), SHARE), :]
                high[i, to, :], low[i, to, :] = two_terms(value)

            done += groups

    def split_either(pair, high, low, i, target):
        if pair[0] == pair[1]:
            split(pair[0], high, low, i, target)
        else:
            for column_of_chips in range(2):
                @pl.when(xh == column_of_chips)
                def _():
                    split(pair[column_of_chips], high, low, i, target)

    def row_target(g):
        return (g % 2 + 2 - c) % 2 * 8 + (g // 4 + 4 - y) % 4 * 2 + (g // 2 % 2 + 2 - xl) % 2

    if before:
        mine[:, :before] = refs[count][...]
        other[:, :before] = refs[count + 1][...]
    for i, pair in enumerate(rows):
        split_either(pair, row_high, row_low, i, row_target)
    for i, pair in enumerate(columns):
        split_either(pair, column_high, column_low, i, lambda g: g)

    def dot(a, b):
        return lax.dot_general(a, b, (((1,), (1,)), ((), ())), preferred_element_type=jnp.float32)

    for t, (r, k) in enumerate(tiles):
        @pl.loop(0, 2)
        def _(half):
            part = pl.ds(pl.multiple_of(half * 256, 256), 256)
            ah, al = row_high[r], row_low[r]
            bh, bl = column_high[k, part, :], column_low[k, part, :]
            v = dot(ah, bh) + dot(ah, bl) + dot(al, bh)
            to = pl.ds(pl.multiple_of(before + t * TILE + half * 256, 256), 256)
            mine[:, to] = v[:256]
            other[:, to] = v[256:]


def products(place_now, tiles, rows, columns, before=()):
    start = before[0].shape[1] if before else 0
    arrays = []

    def index_of(chunk):
        for i, known in enumerate(arrays):
            if known is chunk:
                return i
        arrays.append(chunk)
        return len(arrays) - 1

    number = lambda pair: tuple(tuple(index_of(chunk) for chunk in block) for block in pair)
    rows, columns = [number(pair) for pair in rows], [number(pair) for pair in columns]
    width = start + TILE * len(tiles)
    operand = lambda n: pltpu.VMEM((n, TILE, 1024), jnp.bfloat16)
    return call(
        functools.partial(products_kernel, tiles, rows, columns, len(arrays), start),
        [(256, width)] * 2,
        [place_now, *arrays, *before],
        28,
        [operand(len(rows)), operand(len(rows)), operand(len(columns)), operand(len(columns))],
    )


def cores_kernel(place_ref, mine, got, *outs):
    for r in range(NY):
        rows = pl.ds(r * 64, 64)
        outs[r][...] = mine[rows, :] + got[rows, :]


def ys_kernel(place_ref, kept, a, b, d, mine, other):
    low, high = pl.ds(0, SHARE), pl.ds(SHARE, SHARE)
    mine[...] = kept[low, :] + a[low, :] + b[low, :] + d[low, :]
    other[...] = kept[high, :] + a[high, :] + b[high, :] + d[high, :]


def over_cores(place_now, mine, other):
    return call(cores_kernel, [(64, mine.shape[1])] * NY, [place_now, mine, send(other, swap_core)], 10)


def over_y(place_now, parts):
    got = [send(parts[r], y_by(r)) for r in (1, 3, 2)]
    return call(ys_kernel, [(SHARE, parts[0].shape[1])] * 2, [place_now, parts[0], *got], 4)


def over_x(mine, other):
    return mine + send(other, lambda y, xl, c, z, xh: (y, 1 - xl, c, z, xh))


def body(factors):
    aux, bas = lax.axis_index("aux"), lax.axis_index("bas")
    first = bas % 2 == 0
    place_now = jnp.stack([aux // 4, (aux // 2) % 2, aux % 2, bas % 2]).astype(jnp.int32)
    tie = lax.optimization_barrier
    same = lambda block: (tuple(block), tuple(block))

    own = factors[0]
    halves = own[:256], own[256:]
    o0 = send(own, swap_xh)
    p1 = [send(v, z_by(-1)) for v in halves]
    m1 = [send(v, z_by(1)) for v in halves]
    p1[1], m1[1], o0 = tie((p1[1], m1[1], o0))
    p2 = [send(v, z_by(-1)) for v in p1]
    m2 = [send(v, z_by(1)) for v in m1]

    product1 = products(
        place_now, [(0, 0), (0, 1), (1, 1), (1, 2)], [same([own]), same(m1)], [same([own]), same(p1), same([o0])]
    )
    p2[0], m2[0], product1 = tie((p2[0], m2[0], product1))
    o2 = [send(p2[0], swap_xh)]
    parts1 = over_cores(place_now, *product1)
    p2[1], m2, o2, parts1 = tie((p2[1], m2, o2, parts1))
    o2.append(send(p2[1], swap_xh))
    sums1 = over_y(place_now, parts1)
    product2 = products(place_now, [(0, 0), (0, 1), (0, 2)], [same(m2)], [same(p1), same(p2), same([o0])])
    o2, product2 = tie((o2, product2))
    product2 = products(
        place_now, [(0, 0), (1, 1)], [same(m1), ((own,), tuple(m2))], [same(o2), ((o0,), tuple(o2))], product2
    )
    product2, sums1 = tie((product2, sums1))
    parts2 = over_cores(place_now, *product2)

    v = over_x(*sums1)
    d0, d1, d2, t1 = jnp.split(v, 4, 1)
    d2, t1 = jnp.split(send(v[:, 1024:], z_by(-1)), 2, 1)
    v = over_x(*over_y(place_now, parts2))
    t3 = send(v[:, 1536:2048], z_by(-1))
    x = v[:, 2048:]
    d3, d4, t2, far = jnp.split(send(jnp.concatenate([v[:, :1536], x], 1), z_by(-2)), 4, 1)
    x = jnp.where(first, x, far)

    odd = [jnp.where(first, a, b) for a, b in ((x, t1), (t1, t2), (t2, t3), (t3, x))]
    return jnp.stack([d0, odd[0], d1, odd[1], d2, odd[2], d3, odd[3], d4], axis=1)[None]


def solution(mesh):
    return jax.shard_map(
        body,
        mesh=mesh,
        in_specs=(P("aux", "bas", None),),
        out_specs=P("bas", "aux", None, None),
        check_vma=False,
    )
```

```python
import functools

import jax
import jax.numpy as jnp
from jax import lax
from jax.experimental import pallas as pl
from jax.experimental.pallas import tpu as pltpu
from jax.sharding import PartitionSpec as P

NY, NXL, NC, NZ, NXH = 4, 2, 2, 8, 2
TILE = 512
SHARE = 32
HEAD = 192


def place(y, xl, c, z, xh):
    return (((y % NY) * NXL + xl % NXL) * NC + c % NC) * (NZ * NXH) + (z % NZ) * NXH + xh % NXH


def send(value, target):
    pairs = []
    for y in range(NY):
        for xl in range(NXL):
            for c in range(NC):
                for z in range(NZ):
                    for xh in range(NXH):
                        to = target(y, xl, c, z, xh)
                        if to is not None:
                            pairs.append((place(y, xl, c, z, xh), place(*to)))
    return lax.ppermute(value, ("aux", "bas"), pairs)


def z_by(step):
    return lambda y, xl, c, z, xh: (y, xl, c, z + step, xh)


def y_by(step):
    return lambda y, xl, c, z, xh: (y + step, xl, c, z, xh)


def swap_core(y, xl, c, z, xh):
    return y, xl, 1 - c, z, xh


def swap_xl(y, xl, c, z, xh):
    return y, 1 - xl, c, z, xh


def swap_xh(y, xl, c, z, xh):
    return y, xl, c, z, 1 - xh


def call(kernel, outs, args, vmem, dtype=jnp.float32):
    return pl.pallas_call(
        kernel,
        out_shape=[jax.ShapeDtypeStruct(shape, dtype) for shape in outs],
        in_specs=[pl.BlockSpec(memory_space=pltpu.SMEM)] + [pl.BlockSpec(memory_space=pltpu.VMEM)] * (len(args) - 1),
        out_specs=[pl.BlockSpec(memory_space=pltpu.VMEM)] * len(outs),
        compiler_params=pltpu.CompilerParams(vmem_limit_bytes=vmem * 2**20),
        cost_estimate=pl.CostEstimate(flops=0, bytes_accessed=0, transcendentals=0),
    )(*args)


def two_terms(value):
    high = value.astype(jnp.bfloat16)
    return high, (value - high.astype(jnp.float32)).astype(jnp.bfloat16)


def split_kernel(rows, columns, count, place_ref, *refs):
    operands, outs = refs[:count], refs[count:]
    y, xl, c, xh = (place_ref[i] for i in range(4))

    def split(block, high, low, target):
        done = 0
        for at, first in block:
            chunk = operands[at]
            groups = chunk.shape[0] // SHARE
            depth = high.shape[1]

            @pl.loop(0, groups)
            def _(g, chunk=chunk, done=done, first=first, depth=depth):
                to = pl.ds(pl.multiple_of(target(g + done) * SHARE, SHARE), SHARE)
                value = chunk[pl.ds(pl.multiple_of(g * SHARE, SHARE), SHARE), first:first + depth]
                high[to, :], low[to, :] = two_terms(value)

            done += groups

    def row_target(g):
        return (g % 2 + 2 - c) % 2 * 8 + (g // 4 + 4 - y) % 4 * 2 + (g // 2 % 2 + 2 - xl) % 2

    for i, pair in enumerate(rows + columns):
        target = row_target if i < len(rows) else lambda g: g
        high, low = outs[2 * i], outs[2 * i + 1]
        if pair[0] == pair[1]:
            split(pair[0], high, low, target)
        else:
            for column_of_chips in range(2):
                @pl.when(xh == column_of_chips)
                def _():
                    split(pair[column_of_chips], high, low, target)


def split(place_now, rows, columns, depth=1024):
    arrays = []

    def index_of(chunk):
        for i, known in enumerate(arrays):
            if known is chunk:
                return i
        arrays.append(chunk)
        return len(arrays) - 1

    number = lambda pair: tuple(tuple((index_of(chunk), first) for chunk, first in block) for block in pair)
    rows, columns = [number(pair) for pair in rows], [number(pair) for pair in columns]
    outs = call(
        functools.partial(split_kernel, rows, columns, len(arrays)),
        [(TILE, depth)] * (2 * len(rows + columns)),
        [place_now, *arrays],
        24,
        jnp.bfloat16,
    )
    return [tuple(outs[i:i + 2]) for i in range(0, len(outs), 2)]


def products_kernel(tiles, either, count, before, place_ref, *refs):
    operands, (mine, other) = refs[:count], refs[-2:]
    if before:
        mine[:, :before] = refs[count][...]
        other[:, :before] = refs[count + 1][...]

    def dot(a, b):
        return lax.dot_general(a, b, (((1,), (1,)), ((), ())), preferred_element_type=jnp.float32)

    def write(t, tile):
        rh, rl, ch, cl = tile

        @pl.loop(0, 2)
        def _(half):
            part = pl.ds(pl.multiple_of(half * 256, 256), 256)
            ah, al = operands[rh][...], operands[rl][...]
            bh, bl = operands[ch][part, :], operands[cl][part, :]
            v = dot(ah, bh) + dot(ah, bl) + dot(al, bh)
            to = pl.ds(pl.multiple_of(before + t * TILE + half * 256, 256), 256)
            mine[:, to] = v[:256]
            other[:, to] = v[256:]

    for t, tile in enumerate(tiles):
        write(t, tile)
    for column_of_chips, tile in enumerate(either):
        @pl.when(place_ref[3] == column_of_chips)
        def _():
            write(len(tiles), tile)


def products(place_now, pairs, before=(), either=()):
    arrays = []

    def index_of(array):
        for i, known in enumerate(arrays):
            if known is array:
                return i
        arrays.append(array)
        return len(arrays) - 1

    number = lambda some: [tuple(index_of(array) for array in rows + columns) for rows, columns in some]
    tiles, either = number(pairs), number(either)
    start = before[0].shape[1] if before else 0
    width = start + TILE * (len(tiles) + bool(either))
    kernel = functools.partial(products_kernel, tiles, either, len(arrays), start)
    return call(kernel, [(256, width)] * 2, [place_now, *arrays, *before], 28)


def cores_kernel(place_ref, mine, got, *outs):
    for r in range(NY):
        rows = pl.ds(r * 64, 64)
        outs[r][...] = mine[rows, :] + got[rows, :]


def ys_kernel(place_ref, kept, a, b, d, mine, other):
    low, high = pl.ds(0, SHARE), pl.ds(SHARE, SHARE)
    mine[...] = kept[low, :] + a[low, :] + b[low, :] + d[low, :]
    other[...] = kept[high, :] + a[high, :] + b[high, :] + d[high, :]


def over_cores(place_now, mine, other):
    return call(cores_kernel, [(64, mine.shape[1])] * NY, [place_now, mine, send(other, swap_core)], 10)


def mixed_cores_kernel(width, place_ref, mine, got, *outs):
    by_y, by_x = outs[:NY], outs[NY:]
    for r in range(NY):
        rows = pl.ds(r * 64, 64)
        by_y[r][...] = mine[rows, :width] + got[rows, :width]
        for x in range(NXL):
            rows = pl.ds(r * 64 + x * SHARE, SHARE)
            by_x[x][pl.ds(r * SHARE, SHARE), :] = mine[rows, width:] + got[rows, width:]


def mixed_kernel(place_ref, kept, a, b, d, kept_x, got_x, mine, other, *outs):
    ys_kernel(place_ref, kept, a, b, d, mine, other)
    for r in range(NY):
        rows = pl.ds(r * SHARE, SHARE)
        outs[r][...] = kept_x[rows, :] + got_x[rows, :]


def mixed_sum(place_now, mine, other, width):
    rest = mine.shape[1] - width
    shapes = [(64, width)] * NY + [(NY * SHARE, rest)] * NXL
    outs = call(functools.partial(mixed_cores_kernel, width), shapes, [place_now, mine, send(other, swap_core)], 12)
    by_y, by_x = outs[:NY], outs[NY:]
    got = [send(by_y[r], y_by(r)) for r in (1, 3, 2)] + [by_x[0], send(by_x[1], swap_xl)]
    shapes = [(SHARE, width)] * 2 + [(SHARE, rest)] * NY
    mine, other, *by_y = call(mixed_kernel, shapes, [place_now, by_y[0], *got], 8)
    got = [send(by_y[r], y_by(r)) for r in (1, 3, 2)]
    return mine + send(other, swap_xl), by_y[0] + got[0] + got[1] + got[2]


def over_y(place_now, parts):
    got = [send(parts[r], y_by(r)) for r in (1, 3, 2)]
    return call(ys_kernel, [(SHARE, parts[0].shape[1])] * 2, [place_now, parts[0], *got], 4)


def over_x(mine, other):
    return mine + send(other, swap_xl)


def body(factors):
    aux, bas = lax.axis_index("aux"), lax.axis_index("bas")
    first = bas % 2 == 0
    place_now = jnp.stack([aux // 4, aux // 2 % 2, aux % 2, bas % 2]).astype(jnp.int32)
    tie = lax.optimization_barrier
    whole = lambda *chunks: (tuple((chunk, 0) for chunk in chunks),) * 2

    own = factors[0]
    rows_own, cols_own = split(place_now, [whole(own)], [whole(own)])
    p1, m1, o0 = send(own, z_by(-1)), send(own, z_by(1)), send(own, swap_xh)
    p1, m1, o0, rows_own, cols_own = tie((p1, m1, o0, rows_own, cols_own))

    p1a, p1b, m1a, m1b = p1[:HEAD], p1[HEAD:], m1[:HEAD], m1[HEAD:]
    p2a, m2a = send(p1a, z_by(-1)), send(m1a, z_by(1))
    rows_m1, cols_p1, cols_o0 = split(place_now, [whole(m1)], [whole(p1), whole(o0)])
    product1 = products(
        place_now, [(rows_own, cols_own), (rows_own, cols_p1), (rows_m1, cols_p1), (rows_m1, cols_o0)]
    )
    p2a, m2a, product1, p1b, m1b = tie((p2a, m2a, product1, p1b, m1b))

    p2b, m2b, o2a = send(p1b, z_by(-1)), send(m1b, z_by(1)), send(p2a, swap_xh)
    parts1 = over_cores(place_now, *product1)
    p2b, m2b, o2a, parts1 = tie((p2b, m2b, o2a, parts1))

    o2b = send(p2b, swap_xh)
    sums1 = over_y(place_now, parts1)
    rows_m2, cols_p2 = split(place_now, [whole(m2a, m2b)], [whole(p2a, p2b)])
    product2 = products(place_now, [(rows_m2, cols) for cols in (cols_p1, cols_p2, cols_o0)])
    o2b, product2 = tie((o2b, product2))
    o2 = ((o2a, 0), (o2b, 0))
    (cols_o2,) = split(place_now, [], [(o2, o2)])
    product2 = products(place_now, [(rows_m1, cols_o2)], product2, ((rows_own, cols_o0), (rows_m2, cols_o2)))
    product2, sums1 = tie((product2, sums1))
    far, v = mixed_sum(place_now, *product2, 1536)
    d3, d4, t2 = jnp.split(send(far, z_by(-2)), 3, 1)
    t3, x = send(v[:, :512], z_by(-1)), v[:, 512:]
    x = jnp.where(first, x, send(x, z_by(-2)))

    v = over_x(*sums1)
    d0, d1 = jnp.split(v[:, :1024], 2, 1)
    d2, t1 = jnp.split(send(v[:, 1024:], z_by(-1)), 2, 1)

    odd = [jnp.where(first, a, b) for a, b in ((x, t1), (t1, t2), (t2, t3), (t3, x))]
    return jnp.stack([d0, odd[0], d1, odd[1], d2, odd[2], d3, odd[3], d4], axis=1)[None]


def solution(mesh):
    return jax.shard_map(
        body,
        mesh=mesh,
        in_specs=(P("aux", "bas", None),),
        out_specs=P("bas", "aux", None, None),
        check_vma=False,
    )
```

```python
import functools

import jax
import jax.numpy as jnp
from jax import lax
from jax.experimental import pallas as pl
from jax.experimental.pallas import tpu as pltpu
from jax.sharding import PartitionSpec as P

NY, NXL, NC, NZ, NXH = 4, 2, 2, 8, 2
TILE = 512
SHARE = 32
HALF = 256


def place(y, xl, c, z, xh):
    return (((y % NY) * NXL + xl % NXL) * NC + c % NC) * (NZ * NXH) + (z % NZ) * NXH + xh % NXH


def send(value, target):
    pairs = []
    for y in range(NY):
        for xl in range(NXL):
            for c in range(NC):
                for z in range(NZ):
                    for xh in range(NXH):
                        to = target(y, xl, c, z, xh)
                        if to is not None:
                            pairs.append((place(y, xl, c, z, xh), place(*to)))
    return lax.ppermute(value, ("aux", "bas"), pairs)


def z_by(step):
    return lambda y, xl, c, z, xh: (y, xl, c, z + step, xh)


def y_by(step):
    return lambda y, xl, c, z, xh: (y + step, xl, c, z, xh)


def swap_core(y, xl, c, z, xh):
    return y, xl, 1 - c, z, xh


def swap_xl(y, xl, c, z, xh):
    return y, 1 - xl, c, z, xh


def swap_xh(y, xl, c, z, xh):
    return y, xl, c, z, 1 - xh


def call(kernel, outs, args, vmem, dtype=jnp.float32):
    return pl.pallas_call(
        kernel,
        out_shape=[jax.ShapeDtypeStruct(shape, dtype) for shape in outs],
        in_specs=[pl.BlockSpec(memory_space=pltpu.SMEM)] + [pl.BlockSpec(memory_space=pltpu.VMEM)] * (len(args) - 1),
        out_specs=[pl.BlockSpec(memory_space=pltpu.VMEM)] * len(outs),
        compiler_params=pltpu.CompilerParams(vmem_limit_bytes=vmem * 2**20),
        cost_estimate=pl.CostEstimate(flops=0, bytes_accessed=0, transcendentals=0),
    )(*args)


def two_terms(value):
    high = value.astype(jnp.bfloat16)
    return high, (value - high.astype(jnp.float32)).astype(jnp.bfloat16)


def split_kernel(rows, columns, count, place_ref, *refs):
    operands, outs = refs[:count], refs[count:]
    y, xl, c, xh = (place_ref[i] for i in range(4))

    def split(block, high, low, target):
        done = 0
        for at, first in block:
            chunk = operands[at]
            groups = chunk.shape[0] // SHARE
            depth = high.shape[1]

            @pl.loop(0, groups)
            def _(g, chunk=chunk, done=done, first=first, depth=depth):
                to = pl.ds(pl.multiple_of(target(g + done) * SHARE, SHARE), SHARE)
                value = chunk[pl.ds(pl.multiple_of(g * SHARE, SHARE), SHARE), first:first + depth]
                high[to, :], low[to, :] = two_terms(value)

            done += groups

    def row_target(g):
        return (g % 2 + 2 - c) % 2 * 8 + (g // 4 + 4 - y) % 4 * 2 + (g // 2 % 2 + 2 - xl) % 2

    for i, pair in enumerate(rows + columns):
        target = row_target if i < len(rows) else lambda g: g
        high, low = outs[2 * i], outs[2 * i + 1]
        if pair[0] == pair[1]:
            split(pair[0], high, low, target)
        else:
            for column_of_chips in range(2):
                @pl.when(xh == column_of_chips)
                def _():
                    split(pair[column_of_chips], high, low, target)


def split(place_now, rows, columns, depth=1024):
    arrays = []

    def index_of(chunk):
        for i, known in enumerate(arrays):
            if known is chunk:
                return i
        arrays.append(chunk)
        return len(arrays) - 1

    number = lambda pair: tuple(tuple((index_of(chunk), first) for chunk, first in block) for block in pair)
    rows, columns = [number(pair) for pair in rows], [number(pair) for pair in columns]
    outs = call(
        functools.partial(split_kernel, rows, columns, len(arrays)),
        [(sum(arrays[at].shape[0] for at, _ in pair[0]), depth) for pair in rows + columns for _ in range(2)],
        [place_now, *arrays],
        24,
        jnp.bfloat16,
    )
    return [tuple(outs[i:i + 2]) for i in range(0, len(outs), 2)]


def products_kernel(tiles, either, count, before, place_ref, *refs):
    operands, (mine, other) = refs[:count], refs[-2:]
    if before:
        mine[:, :before] = refs[count][...]
        other[:, :before] = refs[count + 1][...]

    def dot(a, b):
        return lax.dot_general(a, b, (((1,), (1,)), ((), ())), preferred_element_type=jnp.float32)

    def write(at, tile):
        rh, rl, ch, cl = tile

        @pl.loop(0, operands[ch].shape[0] // HALF)
        def _(half):
            part = pl.ds(pl.multiple_of(half * HALF, HALF), HALF)
            ah, al = operands[rh][...], operands[rl][...]
            bh, bl = operands[ch][part, :], operands[cl][part, :]
            v = dot(ah, bh) + dot(ah, bl) + dot(al, bh)
            to = pl.ds(pl.multiple_of(at + half * HALF, HALF), HALF)
            mine[:, to] = v[:256]
            other[:, to] = v[256:]

    at = before
    for tile in tiles:
        write(at, tile)
        at += operands[tile[2]].shape[0]
    for column_of_chips, tile in enumerate(either):
        @pl.when(place_ref[3] == column_of_chips)
        def _():
            write(at, tile)


def products(place_now, pairs, before=(), either=()):
    arrays = []

    def index_of(array):
        for i, known in enumerate(arrays):
            if known is array:
                return i
        arrays.append(array)
        return len(arrays) - 1

    number = lambda some: [tuple(index_of(array) for array in rows + columns) for rows, columns in some]
    tiles, either = number(pairs), number(either)
    start = before[0].shape[1] if before else 0
    width = start + sum(arrays[tile[2]].shape[0] for tile in tiles + either[:1])
    kernel = functools.partial(products_kernel, tiles, either, len(arrays), start)
    return call(kernel, [(256, width)] * 2, [place_now, *arrays, *before], 28)


def cores_kernel(place_ref, mine, got, *outs):
    for r in range(NY):
        rows = pl.ds(r * 64, 64)
        outs[r][...] = mine[rows, :] + got[rows, :]


def ys_kernel(place_ref, kept, a, b, d, mine, other):
    low, high = pl.ds(0, SHARE), pl.ds(SHARE, SHARE)
    mine[...] = kept[low, :] + a[low, :] + b[low, :] + d[low, :]
    other[...] = kept[high, :] + a[high, :] + b[high, :] + d[high, :]


def over_cores(place_now, mine, other):
    return call(cores_kernel, [(64, mine.shape[1])] * NY, [place_now, mine, send(other, swap_core)], 10)


def mixed_cores_kernel(by_y_halves, by_x_halves, place_ref, mine, got, *outs):
    by_y, by_x = outs[:NY], outs[NY:]
    for r in range(NY):
        for i, h in enumerate(by_y_halves):
            rows, from_, to = pl.ds(r * 64, 64), pl.ds(h * HALF, HALF), pl.ds(i * HALF, HALF)
            by_y[r][:, to] = mine[rows, from_] + got[rows, from_]
        for i, h in enumerate(by_x_halves):
            from_, to = pl.ds(h * HALF, HALF), pl.ds(i * HALF, HALF)
            for x in range(NXL):
                rows = pl.ds(r * 64 + x * SHARE, SHARE)
                by_x[x][pl.ds(r * SHARE, SHARE), to] = mine[rows, from_] + got[rows, from_]


def mixed_kernel(place_ref, kept, a, b, d, kept_x, got_x, mine, other, *outs):
    ys_kernel(place_ref, kept, a, b, d, mine, other)
    for r in range(NY):
        rows = pl.ds(r * SHARE, SHARE)
        outs[r][...] = kept_x[rows, :] + got_x[rows, :]


def mixed_sum(place_now, mine, other, by_y_halves, by_x_halves):
    wide, rest = HALF * len(by_y_halves), HALF * len(by_x_halves)
    kernel = functools.partial(mixed_cores_kernel, by_y_halves, by_x_halves)
    shapes = [(64, wide)] * NY + [(NY * SHARE, rest)] * NXL
    outs = call(kernel, shapes, [place_now, mine, send(other, swap_core)], 12)
    by_y, by_x = outs[:NY], outs[NY:]
    got = [send(by_y[r], y_by(r)) for r in (1, 3, 2)] + [by_x[0], send(by_x[1], swap_xl)]
    shapes = [(SHARE, wide)] * 2 + [(SHARE, rest)] * NY
    mine, other, *by_y = call(mixed_kernel, shapes, [place_now, by_y[0], *got], 8)
    first = mine + send(other, swap_xl)
    got = [send(by_y[r], y_by(r)) for r in (1, 3, 2)]
    return first, by_y[0] + got[0] + got[1] + got[2]


def over_x(mine, other):
    return mine + send(other, swap_xl)


def body(factors):
    aux, bas = lax.axis_index("aux"), lax.axis_index("bas")
    first = bas % 2 == 0
    place_now = jnp.stack([aux // 4, aux // 2 % 2, aux % 2, bas % 2]).astype(jnp.int32)
    tie = lax.optimization_barrier
    whole = lambda *chunks: (tuple((chunk, 0) for chunk in chunks),) * 2

    own = factors[0]
    rows_own, cols_own = split(place_now, [whole(own)], [whole(own)])
    p1, m1, o0 = send(own, z_by(-1)), send(own, z_by(1)), send(own, swap_xh)
    p1, m1, o0, rows_own, cols_own = tie((p1, m1, o0, rows_own, cols_own))

    p1a, p1b, m1a, m1b = p1[:HALF], p1[HALF:], m1[:HALF], m1[HALF:]
    p2a, m2a = send(p1a, z_by(-1)), send(m1a, z_by(1))
    rows_m1, cols_p1, cols_o0 = split(place_now, [whole(m1)], [whole(p1), whole(o0)])
    product1 = products(
        place_now, [(rows_own, cols_own), (rows_own, cols_p1), (rows_m1, cols_p1), (rows_m1, cols_o0)]
    )
    p2a, m2a, product1, p1b, m1b = tie((p2a, m2a, product1, p1b, m1b))

    p2b, m2b, o2a = send(p1b, z_by(-1)), send(m1b, z_by(1)), send(p2a, swap_xh)
    parts1 = over_cores(place_now, *product1)
    p2b, m2b, o2a, parts1 = tie((p2b, m2b, o2a, parts1))

    o2b = send(p2b, swap_xh)
    got1 = [send(parts1[r], y_by(r)) for r in (1, 3, 2)]
    rows_m2, cols_p2, cols_o2a = split(place_now, [whole(m2a, m2b)], [whole(p2a, p2b), whole(o2a)])
    cols_o0a, cols_o0b = [[v[start:start + HALF] for v in cols_o0] for start in (0, HALF)]
    product2 = products(
        place_now,
        [(rows_m2, cols_p2), (rows_m2, cols_o0), (rows_m1, cols_p2), (rows_m1, cols_o2a)],
        (),
        ((rows_own, tuple(cols_o0a)), (rows_m2, cols_o2a)),
    )
    o2b, product2 = tie((o2b, product2))
    (cols_o2b,) = split(place_now, [], [whole(o2b)])
    product2 = products(
        place_now, [(rows_m1, cols_o2b)], product2, ((rows_own, tuple(cols_o0b)), (rows_m2, cols_o2b))
    )
    product2, parts1, got1 = tie((product2, parts1, got1))
    far, v = mixed_sum(place_now, *product2, (0, 1, 2, 3, 7, 9), (4, 5, 6, 8))
    x = far[:, 1024:]
    d4, t2, far = jnp.split(send(far, z_by(-2)), 3, 1)
    d3, t3 = jnp.split(send(v, z_by(-1)), 2, 1)
    x = jnp.where(first, x, far)

    v = over_x(*call(ys_kernel, [(SHARE, parts1[0].shape[1])] * 2, [place_now, parts1[0], *got1], 4))
    d0, d1 = jnp.split(v[:, :1024], 2, 1)
    d2, t1 = jnp.split(send(v[:, 1024:], z_by(-1)), 2, 1)

    odd = [jnp.where(first, a, b) for a, b in ((x, t1), (t1, t2), (t2, t3), (t3, x))]
    return jnp.stack([d0, odd[0], d1, odd[1], d2, odd[2], d3, odd[3], d4], axis=1)[None]


def solution(mesh):
    return jax.shard_map(
        body,
        mesh=mesh,
        in_specs=(P("aux", "bas", None),),
        out_specs=P("bas", "aux", None, None),
        check_vma=False,
    )
```

```python
import functools

import jax
import jax.numpy as jnp
from jax import lax
from jax.experimental import pallas as pl
from jax.experimental.pallas import tpu as pltpu
from jax.sharding import PartitionSpec as P

NY, NXL, NC, NZ, NXH = 4, 2, 2, 8, 2
TILE = 512
SHARE = 32
HALF = 256


def place(y, xl, c, z, xh):
    return (((y % NY) * NXL + xl % NXL) * NC + c % NC) * (NZ * NXH) + (z % NZ) * NXH + xh % NXH


def send(value, target):
    pairs = []
    for y in range(NY):
        for xl in range(NXL):
            for c in range(NC):
                for z in range(NZ):
                    for xh in range(NXH):
                        to = target(y, xl, c, z, xh)
                        if to is not None:
                            pairs.append((place(y, xl, c, z, xh), place(*to)))
    return lax.ppermute(value, ("aux", "bas"), pairs)


def z_by(step):
    return lambda y, xl, c, z, xh: (y, xl, c, z + step, xh)


def y_by(step):
    return lambda y, xl, c, z, xh: (y + step, xl, c, z, xh)


def swap_core(y, xl, c, z, xh):
    return y, xl, 1 - c, z, xh


def swap_xl(y, xl, c, z, xh):
    return y, 1 - xl, c, z, xh


def swap_xh(y, xl, c, z, xh):
    return y, xl, c, z, 1 - xh


def call(kernel, outs, args, vmem, dtype=jnp.float32):
    return pl.pallas_call(
        kernel,
        out_shape=[jax.ShapeDtypeStruct(shape, dtype) for shape in outs],
        in_specs=[pl.BlockSpec(memory_space=pltpu.SMEM)] + [pl.BlockSpec(memory_space=pltpu.VMEM)] * (len(args) - 1),
        out_specs=[pl.BlockSpec(memory_space=pltpu.VMEM)] * len(outs),
        compiler_params=pltpu.CompilerParams(vmem_limit_bytes=vmem * 2**20),
        cost_estimate=pl.CostEstimate(flops=0, bytes_accessed=0, transcendentals=0),
    )(*args)


def two_terms(value):
    high = value.astype(jnp.bfloat16)
    return high, (value - high.astype(jnp.float32)).astype(jnp.bfloat16)


def split_kernel(rows, columns, count, place_ref, *refs):
    operands, outs = refs[:count], refs[count:]
    y, xl, c, xh = (place_ref[i] for i in range(4))

    def split(block, high, low, target):
        done = 0
        for at, first in block:
            chunk = operands[at]
            groups = chunk.shape[0] // SHARE
            depth = high.shape[1]

            @pl.loop(0, groups)
            def _(g, chunk=chunk, done=done, first=first, depth=depth):
                to = pl.ds(pl.multiple_of(target(g + done) * SHARE, SHARE), SHARE)
                value = chunk[pl.ds(pl.multiple_of(g * SHARE, SHARE), SHARE), first:first + depth]
                high[to, :], low[to, :] = two_terms(value)

            done += groups

    def row_target(g):
        return (g % 2 + 2 - c) % 2 * 8 + (g // 4 + 4 - y) % 4 * 2 + (g // 2 % 2 + 2 - xl) % 2

    for i, pair in enumerate(rows + columns):
        target = row_target if i < len(rows) else lambda g: g
        high, low = outs[2 * i], outs[2 * i + 1]
        if pair[0] == pair[1]:
            split(pair[0], high, low, target)
        else:
            for column_of_chips in range(2):
                @pl.when(xh == column_of_chips)
                def _():
                    split(pair[column_of_chips], high, low, target)


def split(place_now, rows, columns, depth=1024):
    arrays = []

    def index_of(chunk):
        for i, known in enumerate(arrays):
            if known is chunk:
                return i
        arrays.append(chunk)
        return len(arrays) - 1

    number = lambda pair: tuple(tuple((index_of(chunk), first) for chunk, first in block) for block in pair)
    rows, columns = [number(pair) for pair in rows], [number(pair) for pair in columns]
    outs = call(
        functools.partial(split_kernel, rows, columns, len(arrays)),
        [(sum(arrays[at].shape[0] for at, _ in pair[0]), depth) for pair in rows + columns for _ in range(2)],
        [place_now, *arrays],
        24,
        jnp.bfloat16,
    )
    return [tuple(outs[i:i + 2]) for i in range(0, len(outs), 2)]


def products_kernel(tiles, either, count, before, place_ref, *refs):
    operands, (mine, other) = refs[:count], refs[-2:]
    if before:
        mine[:, :before] = refs[count][...]
        other[:, :before] = refs[count + 1][...]

    def dot(a, b):
        return lax.dot_general(a, b, (((1,), (1,)), ((), ())), preferred_element_type=jnp.float32)

    def write(at, tile):
        rh, rl, ch, cl = tile

        @pl.loop(0, operands[ch].shape[0] // HALF)
        def _(half):
            part = pl.ds(pl.multiple_of(half * HALF, HALF), HALF)
            ah, al = operands[rh][...], operands[rl][...]
            bh, bl = operands[ch][part, :], operands[cl][part, :]
            v = dot(ah, bh) + dot(ah, bl) + dot(al, bh)
            to = pl.ds(pl.multiple_of(at + half * HALF, HALF), HALF)
            mine[:, to] = v[:256]
            other[:, to] = v[256:]

    at = before
    for tile in tiles:
        write(at, tile)
        at += operands[tile[2]].shape[0]
    for column_of_chips, tile in enumerate(either):
        @pl.when(place_ref[3] == column_of_chips)
        def _():
            write(at, tile)


def products(place_now, pairs, before=(), either=()):
    arrays = []

    def index_of(array):
        for i, known in enumerate(arrays):
            if known is array:
                return i
        arrays.append(array)
        return len(arrays) - 1

    number = lambda some: [tuple(index_of(array) for array in rows + columns) for rows, columns in some]
    tiles, either = number(pairs), number(either)
    start = before[0].shape[1] if before else 0
    width = start + sum(arrays[tile[2]].shape[0] for tile in tiles + either[:1])
    kernel = functools.partial(products_kernel, tiles, either, len(arrays), start)
    return call(kernel, [(256, width)] * 2, [place_now, *arrays, *before], 28)


def cores_kernel(place_ref, mine, got, *outs):
    for r in range(NY):
        rows = pl.ds(r * 64, 64)
        outs[r][...] = mine[rows, :] + got[rows, :]


def ys_kernel(place_ref, kept, a, b, d, mine, other):
    low, high = pl.ds(0, SHARE), pl.ds(SHARE, SHARE)
    mine[...] = kept[low, :] + a[low, :] + b[low, :] + d[low, :]
    other[...] = kept[high, :] + a[high, :] + b[high, :] + d[high, :]


def over_cores(place_now, mine, other):
    return call(cores_kernel, [(64, mine.shape[1])] * NY, [place_now, mine, send(other, swap_core)], 10)


def mixed_cores_kernel(by_y_halves, by_x_halves, place_ref, mine, got, *outs):
    by_y, by_x = outs[:NY], outs[NY:]
    for r in range(NY):
        for i, h in enumerate(by_y_halves):
            rows, from_, to = pl.ds(r * 64, 64), pl.ds(h * HALF, HALF), pl.ds(i * HALF, HALF)
            by_y[r][:, to] = mine[rows, from_] + got[rows, from_]
        for i, h in enumerate(by_x_halves):
            from_, to = pl.ds(h * HALF, HALF), pl.ds(i * HALF, HALF)
            for x in range(NXL):
                rows = pl.ds(r * 64 + x * SHARE, SHARE)
                by_x[x][pl.ds(r * SHARE, SHARE), to] = mine[rows, from_] + got[rows, from_]


def mixed_kernel(place_ref, kept, a, b, d, kept_x, got_x, mine, other, *outs):
    ys_kernel(place_ref, kept, a, b, d, mine, other)
    for r in range(NY):
        rows = pl.ds(r * SHARE, SHARE)
        outs[r][...] = kept_x[rows, :] + got_x[rows, :]


def mixed_sum(place_now, mine, other, by_y_halves, by_x_halves):
    wide, rest = HALF * len(by_y_halves), HALF * len(by_x_halves)
    kernel = functools.partial(mixed_cores_kernel, by_y_halves, by_x_halves)
    shapes = [(64, wide)] * NY + [(NY * SHARE, rest)] * NXL
    outs = call(kernel, shapes, [place_now, mine, send(other, swap_core)], 12)
    by_y, by_x = outs[:NY], outs[NY:]
    got = [send(by_y[r], y_by(r)) for r in (2, 1, 3)] + [by_x[0], send(by_x[1], swap_xl)]
    shapes = [(SHARE, wide)] * 2 + [(SHARE, rest)] * NY
    mine, other, *by_y = call(mixed_kernel, shapes, [place_now, by_y[0], *got], 8)
    first = mine + send(other, swap_xl)
    got = [send(by_y[r], y_by(r)) for r in (2, 1, 3)]
    return first, by_y[0] + got[0] + got[1] + got[2]


def over_x(mine, other):
    return mine + send(other, swap_xl)


def body(factors):
    aux, bas = lax.axis_index("aux"), lax.axis_index("bas")
    first = bas % 2 == 0
    place_now = jnp.stack([aux // 4, aux // 2 % 2, aux % 2, bas % 2]).astype(jnp.int32)
    tie = lax.optimization_barrier
    whole = lambda *chunks: (tuple((chunk, 0) for chunk in chunks),) * 2

    own = factors[0]
    rows_own, cols_own = split(place_now, [whole(own)], [whole(own)])
    p1, m1, o0 = send(own, z_by(-1)), send(own, z_by(1)), send(own, swap_xh)
    p1, m1, o0, rows_own, cols_own = tie((p1, m1, o0, rows_own, cols_own))

    p1a, p1b, m1a, m1b = p1[:HALF], p1[HALF:], m1[:HALF], m1[HALF:]
    p2a, m2a = send(p1a, z_by(-1)), send(m1a, z_by(1))
    rows_m1, cols_p1, cols_o0 = split(place_now, [whole(m1)], [whole(p1), whole(o0)])
    product1 = products(
        place_now, [(rows_own, cols_own), (rows_own, cols_p1), (rows_m1, cols_p1), (rows_m1, cols_o0)]
    )
    p2a, m2a, product1, p1b, m1b = tie((p2a, m2a, product1, p1b, m1b))

    p2b, m2b, o2a = send(p1b, z_by(-1)), send(m1b, z_by(1)), send(p2a, swap_xh)
    parts1 = over_cores(place_now, *product1)
    p2b, m2b, o2a, parts1 = tie((p2b, m2b, o2a, parts1))

    o2b = send(p2b, swap_xh)
    got1 = [send(parts1[r], y_by(r)) for r in (1, 3, 2)]
    rows_m2, rows_p2, cols_m2, cols_p2, cols_o2a = split(
        place_now, [whole(m2a, m2b), whole(p2a, p2b)], [whole(m2a, m2b), whole(p2a, p2b), whole(o2a)]
    )
    cols_o0a, cols_o0b = [[v[start:start + HALF] for v in cols_o0] for start in (0, HALF)]
    product2 = products(
        place_now,
        [(rows_p2, cols_m2), (rows_m2, cols_o0), (rows_m1, cols_p2), (rows_m1, cols_o2a)],
        (),
        ((rows_own, tuple(cols_o0a)), (rows_m2, cols_o2a)),
    )
    o2b, product2 = tie((o2b, product2))
    (cols_o2b,) = split(place_now, [], [whole(o2b)])
    product2 = products(
        place_now, [(rows_m1, cols_o2b)], product2, ((rows_own, tuple(cols_o0b)), (rows_m2, cols_o2b))
    )
    product2, parts1, got1 = tie((product2, parts1, got1))
    far, v = mixed_sum(place_now, *product2, (0, 1, 2, 3, 7, 9), (4, 5, 6, 8))
    x = far[:, 1024:]
    d4 = send(far[:, :512], z_by(2))
    t2, far = jnp.split(send(far[:, 512:], z_by(-2)), 2, 1)
    d3, t3 = jnp.split(send(v, z_by(-1)), 2, 1)
    x = jnp.where(first, x, far)

    v = over_x(*call(ys_kernel, [(SHARE, parts1[0].shape[1])] * 2, [place_now, parts1[0], *got1], 4))
    d0, d1 = jnp.split(v[:, :1024], 2, 1)
    d2, t1 = jnp.split(send(v[:, 1024:], z_by(-1)), 2, 1)

    odd = [jnp.where(first, a, b) for a, b in ((x, t1), (t1, t2), (t2, t3), (t3, x))]
    return jnp.stack([d0, odd[0], d1, odd[1], d2, odd[2], d3, odd[3], d4], axis=1)[None]


def solution(mesh):
    return jax.shard_map(
        body,
        mesh=mesh,
        in_specs=(P("aux", "bas", None),),
        out_specs=P("bas", "aux", None, None),
        check_vma=False,
    )
```

```python
import functools

import jax
import jax.numpy as jnp
from jax import lax
from jax.experimental import pallas as pl
from jax.experimental.pallas import tpu as pltpu
from jax.sharding import PartitionSpec as P

NY, NXL, NC, NZ, NXH = 4, 2, 2, 8, 2
TILE = 512
SHARE = 32
HALF = 256


def place(y, xl, c, z, xh):
    return (((y % NY) * NXL + xl % NXL) * NC + c % NC) * (NZ * NXH) + (z % NZ) * NXH + xh % NXH


def send(value, target):
    pairs = []
    for y in range(NY):
        for xl in range(NXL):
            for c in range(NC):
                for z in range(NZ):
                    for xh in range(NXH):
                        to = target(y, xl, c, z, xh)
                        if to is not None:
                            pairs.append((place(y, xl, c, z, xh), place(*to)))
    return lax.ppermute(value, ("aux", "bas"), pairs)


def z_by(step):
    return lambda y, xl, c, z, xh: (y, xl, c, z + step, xh)


def y_by(step):
    return lambda y, xl, c, z, xh: (y + step, xl, c, z, xh)


def swap_core(y, xl, c, z, xh):
    return y, xl, 1 - c, z, xh


def swap_xl(y, xl, c, z, xh):
    return y, 1 - xl, c, z, xh


def swap_xh(y, xl, c, z, xh):
    return y, xl, c, z, 1 - xh


def call(kernel, outs, args, vmem, dtype=jnp.float32):
    return pl.pallas_call(
        kernel,
        out_shape=[jax.ShapeDtypeStruct(shape, dtype) for shape in outs],
        in_specs=[pl.BlockSpec(memory_space=pltpu.SMEM)] + [pl.BlockSpec(memory_space=pltpu.VMEM)] * (len(args) - 1),
        out_specs=[pl.BlockSpec(memory_space=pltpu.VMEM)] * len(outs),
        compiler_params=pltpu.CompilerParams(vmem_limit_bytes=vmem * 2**20),
        cost_estimate=pl.CostEstimate(flops=0, bytes_accessed=0, transcendentals=0),
    )(*args)


def two_terms(value):
    high = value.astype(jnp.bfloat16)
    return high, (value - high.astype(jnp.float32)).astype(jnp.bfloat16)


def split_kernel(rows, columns, count, place_ref, *refs):
    operands, outs = refs[:count], refs[count:]
    y, xl, c, xh = (place_ref[i] for i in range(4))

    def split(block, high, low, target):
        done = 0
        for at, first in block:
            chunk = operands[at]
            groups = chunk.shape[0] // SHARE
            depth = high.shape[1]

            @pl.loop(0, groups)
            def _(g, chunk=chunk, done=done, first=first, depth=depth):
                to = pl.ds(pl.multiple_of(target(g + done) * SHARE, SHARE), SHARE)
                value = chunk[pl.ds(pl.multiple_of(g * SHARE, SHARE), SHARE), first:first + depth]
                high[to, :], low[to, :] = two_terms(value)

            done += groups

    def row_target(g):
        return (g % 2 + 2 - c) % 2 * 8 + (g // 4 + 4 - y) % 4 * 2 + (g // 2 % 2 + 2 - xl) % 2

    for i, pair in enumerate(rows + columns):
        target = row_target if i < len(rows) else lambda g: g
        high, low = outs[2 * i], outs[2 * i + 1]
        if pair[0] == pair[1]:
            split(pair[0], high, low, target)
        else:
            for column_of_chips in range(2):
                @pl.when(xh == column_of_chips)
                def _():
                    split(pair[column_of_chips], high, low, target)


def split(place_now, rows, columns, depth=1024):
    arrays = []

    def index_of(chunk):
        for i, known in enumerate(arrays):
            if known is chunk:
                return i
        arrays.append(chunk)
        return len(arrays) - 1

    number = lambda pair: tuple(tuple((index_of(chunk), first) for chunk, first in block) for block in pair)
    rows, columns = [number(pair) for pair in rows], [number(pair) for pair in columns]
    outs = call(
        functools.partial(split_kernel, rows, columns, len(arrays)),
        [(sum(arrays[at].shape[0] for at, _ in pair[0]), depth) for pair in rows + columns for _ in range(2)],
        [place_now, *arrays],
        24,
        jnp.bfloat16,
    )
    return [tuple(outs[i:i + 2]) for i in range(0, len(outs), 2)]


def products_kernel(tiles, either, count, before, place_ref, *refs):
    operands, (mine, other) = refs[:count], refs[-2:]
    if before:
        mine[:, :before] = refs[count][...]
        other[:, :before] = refs[count + 1][...]

    def dot(a, b):
        return lax.dot_general(a, b, (((1,), (1,)), ((), ())), preferred_element_type=jnp.float32)

    def write(at, tile):
        rh, rl, ch, cl = tile

        @pl.loop(0, operands[ch].shape[0] // HALF)
        def _(half):
            part = pl.ds(pl.multiple_of(half * HALF, HALF), HALF)
            ah, al = operands[rh][...], operands[rl][...]
            bh, bl = operands[ch][part, :], operands[cl][part, :]
            v = dot(ah, bh) + dot(ah, bl) + dot(al, bh)
            to = pl.ds(pl.multiple_of(at + half * HALF, HALF), HALF)
            mine[:, to] = v[:256]
            other[:, to] = v[256:]

    at = before
    for tile in tiles:
        write(at, tile)
        at += operands[tile[2]].shape[0]
    for column_of_chips, tile in enumerate(either):
        @pl.when(place_ref[3] == column_of_chips)
        def _():
            write(at, tile)


def products(place_now, pairs, before=(), either=()):
    arrays = []

    def index_of(array):
        for i, known in enumerate(arrays):
            if known is array:
                return i
        arrays.append(array)
        return len(arrays) - 1

    number = lambda some: [tuple(index_of(array) for array in rows + columns) for rows, columns in some]
    tiles, either = number(pairs), number(either)
    start = before[0].shape[1] if before else 0
    width = start + sum(arrays[tile[2]].shape[0] for tile in tiles + either[:1])
    kernel = functools.partial(products_kernel, tiles, either, len(arrays), start)
    return call(kernel, [(256, width)] * 2, [place_now, *arrays, *before], 28)


def cores_kernel(place_ref, mine, got, *outs):
    for r in range(NY):
        rows = pl.ds(r * 64, 64)
        outs[r][...] = mine[rows, :] + got[rows, :]


def ys_kernel(place_ref, kept, a, b, d, mine, other):
    low, high = pl.ds(0, SHARE), pl.ds(SHARE, SHARE)
    mine[...] = kept[low, :] + a[low, :] + b[low, :] + d[low, :]
    other[...] = kept[high, :] + a[high, :] + b[high, :] + d[high, :]


def over_cores(place_now, mine, other):
    return call(cores_kernel, [(64, mine.shape[1])] * NY, [place_now, mine, send(other, swap_core)], 10)


def mixed_cores_kernel(by_y_halves, by_x_halves, place_ref, mine, got, *outs):
    by_y, by_x = outs[:NY], outs[NY:]
    for r in range(NY):
        for i, h in enumerate(by_y_halves):
            rows, from_, to = pl.ds(r * 64, 64), pl.ds(h * HALF, HALF), pl.ds(i * HALF, HALF)
            by_y[r][:, to] = mine[rows, from_] + got[rows, from_]
        for i, h in enumerate(by_x_halves):
            from_, to = pl.ds(h * HALF, HALF), pl.ds(i * HALF, HALF)
            for x in range(NXL):
                rows = pl.ds(r * 64 + x * SHARE, SHARE)
                by_x[x][pl.ds(r * SHARE, SHARE), to] = mine[rows, from_] + got[rows, from_]


def mixed_kernel(place_ref, kept, a, b, d, kept_x, got_x, mine, other, *outs):
    ys_kernel(place_ref, kept, a, b, d, mine, other)
    for r in range(NY):
        rows = pl.ds(r * SHARE, SHARE)
        outs[r][...] = kept_x[rows, :] + got_x[rows, :]


def mixed_sum(place_now, mine, other, by_y_halves, by_x_halves):
    wide, rest = HALF * len(by_y_halves), HALF * len(by_x_halves)
    kernel = functools.partial(mixed_cores_kernel, by_y_halves, by_x_halves)
    shapes = [(64, wide)] * NY + [(NY * SHARE, rest)] * NXL
    outs = call(kernel, shapes, [place_now, mine, send(other, swap_core)], 12)
    by_y, by_x = outs[:NY], outs[NY:]
    got = [send(by_y[r], y_by(r)) for r in (2, 1, 3)] + [by_x[0], send(by_x[1], swap_xl)]
    shapes = [(SHARE, wide)] * 2 + [(SHARE, rest)] * NY
    mine, other, *by_y = call(mixed_kernel, shapes, [place_now, by_y[0], *got], 8)
    first = mine + send(other, swap_xl)
    got = [send(by_y[r], y_by(r)) for r in (2, 1, 3)]
    return first, by_y[0] + got[0] + got[1] + got[2]


def over_x(mine, other):
    return mine + send(other, swap_xl)


def body(factors):
    aux, bas = lax.axis_index("aux"), lax.axis_index("bas")
    first = bas % 2 == 0
    place_now = jnp.stack([aux // 4, aux // 2 % 2, aux % 2, bas % 2]).astype(jnp.int32)
    tie = lax.optimization_barrier
    whole = lambda *chunks: (tuple((chunk, 0) for chunk in chunks),) * 2

    own = factors[0]
    rows_own, cols_own = split(place_now, [whole(own)], [whole(own)])
    p1, m1, o0 = send(own, z_by(-1)), send(own, z_by(1)), send(own, swap_xh)
    p1, m1, o0, rows_own, cols_own = tie((p1, m1, o0, rows_own, cols_own))

    p1a, p1b, m1a, m1b = p1[:HALF], p1[HALF:], m1[:HALF], m1[HALF:]
    p2a, m2a = send(p1a, z_by(-1)), send(m1a, z_by(1))
    rows_m1, cols_p1, cols_o0 = split(place_now, [whole(m1)], [whole(p1), whole(o0)])
    product1 = products(
        place_now, [(rows_own, cols_own), (rows_own, cols_p1), (rows_m1, cols_p1), (rows_m1, cols_o0)]
    )
    p2a, m2a, product1, p1b, m1b = tie((p2a, m2a, product1, p1b, m1b))

    p2b, m2b, o2a = send(p1b, z_by(-1)), send(m1b, z_by(1)), send(p2a, swap_xh)
    parts1 = over_cores(place_now, *product1)
    p2b, m2b, o2a, parts1 = tie((p2b, m2b, o2a, parts1))

    o2b = send(p2b, swap_xh)
    got1 = [send(parts1[r], y_by(r)) for r in (1, 3, 2)]
    rows_m2, rows_p2, cols_m2, cols_p2, cols_o2a = split(
        place_now, [whole(m2a, m2b), whole(p2a, p2b)], [whole(m2a, m2b), whole(p2a, p2b), whole(o2a)]
    )
    cols_o0a, cols_o0b = [[v[start:start + HALF] for v in cols_o0] for start in (0, HALF)]
    product2 = products(
        place_now,
        [(rows_p2, cols_m2), (rows_m2, cols_o0), (rows_m1, cols_p2), (rows_m1, cols_o2a)],
        (),
        ((rows_own, tuple(cols_o0a)), (rows_m2, cols_o2a)),
    )
    o2b, product2 = tie((o2b, product2))
    (cols_o2b,) = split(place_now, [], [whole(o2b)])
    product2 = products(
        place_now, [(rows_m1, cols_o2b)], product2, ((rows_own, tuple(cols_o0b)), (rows_m2, cols_o2b))
    )
    product2, parts1, got1 = tie((product2, parts1, got1))
    far, v = mixed_sum(place_now, *product2, (0, 2, 3, 7, 9), (4, 5, 6, 8, 1))
    x = far[:, 768:]
    d4 = send(jnp.concatenate([far[:, :256], v[:, 1024:]], 1), z_by(2))
    t2, far = jnp.split(send(far[:, 256:], z_by(-2)), 2, 1)
    d3, t3 = jnp.split(send(v[:, :1024], z_by(-1)), 2, 1)
    x = jnp.where(first, x, far)

    v = over_x(*call(ys_kernel, [(SHARE, parts1[0].shape[1])] * 2, [place_now, parts1[0], *got1], 4))
    d0, d1 = jnp.split(v[:, :1024], 2, 1)
    d2, t1 = jnp.split(send(v[:, 1024:], z_by(-1)), 2, 1)

    odd = [jnp.where(first, a, b) for a, b in ((x, t1), (t1, t2), (t2, t3), (t3, x))]
    return jnp.stack([d0, odd[0], d1, odd[1], d2, odd[2], d3, odd[3], d4], axis=1)[None]


def solution(mesh):
    return jax.shard_map(
        body,
        mesh=mesh,
        in_specs=(P("aux", "bas", None),),
        out_specs=P("bas", "aux", None, None),
        check_vma=False,
    )
```
